512 devices in a mesh: row: 16 (over z), col: 32 (over x, y, core).
Axes of the slice: x: 4, y: 4, z: 16, core: 2. Of those that a mesh axis runs over, the one named last changes fastest.
Arguments:
- band: float32 [12288, 24576], P('col', 'row'), may hold values from -6 to 6
- band_pattern: int32 [96, 192], P('col', 'row'), may hold values 0 or 1
- slab: float32 [24576, 8192], P('col', 'row'), may hold values from -0.25 to 0.25
- slab_pattern: int32 [192, 64], P('col', 'row'), may hold values 0 or 1
Outputs:
- product: float32 [12288, 8192], P('col', 'row')
The draws below stay inside these ranges and needn't reach their ends.
All inputs are finite; a program needn't handle non-finite values. No bound on the sum of `band_pattern` or of `slab_pattern` on one device may be relied on, other than what follows from the above.
Results may differ from the reference program's by a relative error of at most 0.0003.
Values sent between devices are 32-bit elements; how exact they have to be, the bound alone decides.
A program may use at most 64 MiB of HBM per device.

```python
import jax
import jax.numpy as jnp
from jax import lax

BS = 128
IB = 3
KB = 6
STEPS = 3
MBLK = 96
KBLK = 192
NBLK = 64
N_COL = 32


def set_ends(values, rng, smallest, high):
    shape = values.shape
    place = [jax.random.randint(jax.random.fold_in(rng, axis), (), 0, shape[axis]) for axis in range(len(shape))]
    values = values.at[tuple(place)].set(smallest)
    longest = shape.index(max(shape))
    place[longest] = (place[longest] + 1) % shape[longest]
    return values.at[tuple(place)].set(high)


def block_levels(stream_key, extent, cuts, low, top_value):
    gain, own = 1.0, jax.random.fold_in(stream_key, 6)
    for axis_at, blocks in cuts:
        draws = jnp.exp(jax.random.uniform(jax.random.fold_in(own, axis_at), (blocks,), jnp.float32, low / len(cuts), top_value / len(cuts)))
        gain = gain * jnp.repeat(draws, extent[axis_at] // blocks).reshape([-1 if axis == axis_at else 1 for axis in range(len(extent))])
    return gain


def gaussian(own_key, extent, spread, limit, split=(), kind=jnp.bfloat16):
    entries = jax.random.normal(own_key, extent, jnp.float32) * spread
    if len(split) > 0:
        entries = block_levels(own_key, extent, split, -0.22, 0.18) * entries
    return jnp.clip(entries, min=-limit, max=limit).astype(kind)


def setup_inputs(seed: int = 0) -> dict:
    key_of = jax.random.split(jax.random.key(seed), 5)
    return {
        "band": gaussian(key_of[0], (MBLK * BS, KBLK * BS), 1.0, 6.0, ((0, 32), (1, 16)), jnp.float32),
        "band_pattern": set_ends((jax.random.randint(key_of[1], (MBLK, KBLK), 0, 2) < 1).astype(jnp.int32), jax.random.fold_in(key_of[1], 1), 0, 1),
        "slab": gaussian(key_of[2], (KBLK * BS, NBLK * BS), (STEPS * KB * BS // 4) ** -0.5, 0.25, ((0, 32), (1, 16)), jnp.float32),
        "slab_pattern": set_ends((jax.random.randint(key_of[3], (KBLK, NBLK), 0, 2) < 1).astype(jnp.int32), jax.random.fold_in(key_of[3], 1), 0, 1),
    }


def masked_blocks(values, pattern, rows, cols):
    shaped = values.reshape(rows, BS, cols, BS)
    weights = pattern.astype(jnp.float32)[:, None, :, None]
    return (shaped * weights).reshape(rows * BS, cols * BS)


def reference(band, band_pattern, slab, slab_pattern):
    groups = N_COL

    def one_group(group_index):
        row_start = (group_index * IB * BS).astype(jnp.int32)
        band_rows = lax.dynamic_slice_in_dim(band, row_start, IB * BS, 0)
        pattern_rows = lax.dynamic_slice_in_dim(band_pattern, (group_index * IB).astype(jnp.int32), IB, 0)
        total = jnp.zeros((IB * BS, NBLK * BS), jnp.float32)
        for step in range(STEPS):
            inner = ((group_index + step) % groups).astype(jnp.int32)
            left = lax.dynamic_slice_in_dim(band_rows, (inner * KB * BS).astype(jnp.int32), KB * BS, 1)
            left_pattern = lax.dynamic_slice_in_dim(pattern_rows, (inner * KB).astype(jnp.int32), KB, 1)
            left = masked_blocks(left, left_pattern, IB, KB)
            right = lax.dynamic_slice_in_dim(slab, (inner * KB * BS).astype(jnp.int32), KB * BS, 0)
            right_pattern = lax.dynamic_slice_in_dim(slab_pattern, (inner * KB).astype(jnp.int32), KB, 0)
            right = masked_blocks(right, right_pattern, KB, NBLK)
            total = total + jnp.dot(left, right, preferred_element_type=jnp.float32, precision=lax.Precision.HIGHEST)
        return total

    stacked = lax.map(one_group, jnp.arange(groups, dtype=jnp.int32))
    return stacked.reshape(groups * IB * BS, NBLK * BS)
```

```python
import functools

import jax
import jax.numpy as jnp
from jax import lax
from jax.experimental import pallas as pl
from jax.experimental.pallas import tpu as pltpu
from jax.sharding import PartitionSpec as P

STEPS = 3
BLOCK = 128
PARTS = 4
ROWS = 8
OWN = 18
LAG = 3
LAGX = 1
FEEDS = 8
RELAY_AT = 20
RELAY_EVERY = 5
PASS_FROM = 22
PASS_EVERY = 2
PASS_LATE = 41
VMEM_MIB = 53
MESH = pl.DeviceIdType.MESH


def kernel(
    rows_n,
    cols_n,
    band_ref,
    band_pattern_ref,
    slab_ref,
    slab_pattern_ref,
    out_ref,
    left,
    carry,
    right,
    through,
    right_hi,
    right_lo,
    band_keep,
    slab_keep,
    load_sem,
    stream_recv,
    up_send,
    down_send,
    side_send,
    spread_send,
    side_recv,
    slab_send,
    slab_recv,
    through_send,
    through_recv,
    pass_send,
    pass_recv,
):
    row = lax.axis_index("row")
    col = lax.axis_index("col")
    height, depth = left.shape[1], left.shape[2]
    width = right.shape[2]
    per_holder = band_ref.shape[1] // depth
    across = cols_n // PARTS
    chunks = [OWN] + [carry.shape[2] // ROWS] * (PARTS - 1)
    begins = [0] + [OWN * ROWS + k * carry.shape[2] for k in range(PARTS - 1)]
    slots = max(chunks)
    core = lax.rem(col, 2)
    place = lax.rem(lax.div(col, 2), PARTS)
    sibling = col + 1 - 2 * core

    def column(offset):
        return lax.rem(col + (offset + cols_n), cols_n)

    up = lax.rem(row + 1, rows_n)
    down = lax.rem(row + rows_n - 1, rows_n)

    barrier = pltpu.get_barrier_semaphore()

    def greet(device):
        pl.semaphore_signal(barrier, inc=1, device_id=device, device_id_type=MESH)

    greet((up, col))
    greet((down, col))
    greet((row, sibling))
    greet((row, column(-2)))
    greet((row, column(2)))
    for k in range(1, PARTS):
        greet((row, column(across * k)))
    for where, offsets in ((0, (-6, -4, 6)), (1, (4, 6)), (2, (4,)), (3, (-6, -4))):

        @pl.when(place == where)
        def _():
            for offset in offsets:
                greet((row, column(offset)))

    greetings = 8 + jnp.where(place == 0, 3, jnp.where(place == 2, 1, 2))

    inner, away = [], {}
    reach = [rows_n // 2, rows_n // 2 - 1 + core, rows_n // 2 - 1]
    for s in range(STEPS):
        for i in range(PARTS):
            group = lax.rem(column(-across * i) + s, cols_n)
            away[i, s] = lax.rem(row - lax.div(group, per_holder) + rows_n, rows_n)
            if i == 0:
                inner.append(lax.rem(group, per_holder))

    def piece_load(s):
        return pltpu.make_async_copy(
            band_ref.at[:, pl.ds(pl.multiple_of(inner[s] * depth, depth), depth)],
            left.at[s],
            load_sem.at[s],
        )

    def other_loads():
        return (
            pltpu.make_async_copy(slab_ref, right.at[0], load_sem.at[STEPS]),
            pltpu.make_async_copy(band_pattern_ref, band_keep, load_sem.at[STEPS + 1]),
            pltpu.make_async_copy(slab_pattern_ref, slab_keep, load_sem.at[STEPS + 2]),
        )

    for s in range(STEPS):

        @pl.when(away[0, s] == 0)
        def _():
            piece_load(s).start()

    for copy in other_loads():
        copy.start()
    for copy in other_loads()[1:]:
        copy.wait()

    for s in range(STEPS):

        @pl.when(away[0, s] == 0)
        def _():
            piece_load(s).wait()
            for p in range(height // BLOCK):
                for q in range(depth // BLOCK):
                    keep = band_keep[p, inner[s] * (depth // BLOCK) + q]
                    at = (s, pl.ds(p * BLOCK, BLOCK), pl.ds(q * BLOCK, BLOCK))
                    left[at] = left[at] * keep.astype(jnp.float32)

    pl.semaphore_wait(barrier, greetings)

    def held(i, s, j, count=1):
        if i == 0:
            return left.at[s, pl.ds(pl.multiple_of(j * ROWS, ROWS), count * ROWS)]
        return carry.at[
            i - 1, s, pl.ds(pl.multiple_of(j * ROWS, ROWS), count * ROWS)
        ]

    def settled(i, s, j, count=1):
        at = pl.ds(pl.multiple_of(begins[i] + j * ROWS, ROWS), count * ROWS)
        return left.at[s, at]

    def remote(source, target, send, recv, device):
        return pltpu.make_async_remote_copy(
            src_ref=source,
            dst_ref=target,
            send_sem=send,
            recv_sem=recv,
            device_id=device,
            device_id_type=MESH,
        )

    def lift(i, s, j, count=1):
        block = held(i, s, j, count)
        return remote(
            block, block, up_send.at[i, s], stream_recv.at[i, s, j], (up, col)
        )

    def lower(i, s, j, count=1):
        block = held(i, s, j, count)
        return remote(
            block, block, down_send.at[i, s], stream_recv.at[i, s, j], (down, col)
        )

    def deliver(i, s, j, count=1):
        return remote(
            held(i, s, j, count),
            settled(i, s, j, count),
            side_send.at[i - 1, s],
            side_recv.at[i - 1, s],
            (row, column(-across * i)),
        )

    def spread(i, s, j, count=1):
        return remote(
            settled(i, s, j, count),
            held(i, s, j, count),
            spread_send.at[i - 1, s],
            stream_recv.at[i, s, j],
            (row, column(across * i)),
        )

    for s in range(STEPS):

        @pl.when(away[0, s] == 0)
        def _():
            for j in range(slots):
                for i in range(1, PARTS):
                    if j < chunks[i]:
                        spread(i, s, j).start()

    feed = right.shape[1] // FEEDS
    per_way = FEEDS // PARTS

    def slab_rows(m):
        return pl.ds(m * feed, feed)

    def slab_direct(m):
        return remote(
            right.at[0, slab_rows(m)],
            right.at[2, slab_rows(m)],
            slab_send.at[m],
            slab_recv.at[m],
            (row, column(-2)),
        )

    def slab_out(m):
        way = m // per_way
        return remote(
            right.at[0, slab_rows(m)],
            through.at[m % per_way],
            slab_send.at[m],
            through_recv.at[m % per_way],
            (row, column(2 * way - across)),
        )

    def slab_on(way, n):
        m = way * per_way + n
        return remote(
            through.at[n],
            right.at[2, slab_rows(m)],
            through_send.at[n],
            slab_recv.at[m],
            (row, column(across - 2 - 2 * way)),
        )

    def slab_pass(m, source):
        return remote(
            right.at[source, slab_rows(m)],
            right.at[1, slab_rows(m)],
            pass_send.at[m],
            pass_recv.at[m],
            (row, sibling),
        )

    other_loads()[0].wait()

    def feed_slab(m):
        for p in range(m * feed // BLOCK, -(-(m + 1) * feed // BLOCK)):
            first, last = max(m * feed, p * BLOCK), min((m + 1) * feed, (p + 1) * BLOCK)
            for n in range(width // BLOCK):
                keep = slab_keep[n, p]
                at = (0, pl.ds(first, last - first), pl.ds(n * BLOCK, BLOCK))
                right[at] = right[at] * keep.astype(jnp.float32)
        if m >= FEEDS - per_way:
            slab_direct(m).start()
        else:

            @pl.when(place == 0)
            def _():
                slab_out(m).start()

            @pl.when(place > 0)
            def _():
                slab_direct(m).start()

        @pl.when(core == 1)
        def _():
            slab_pass(m, 0).start()

    def split(s):
        value = right[s]
        high = value.astype(jnp.bfloat16)
        right_hi[s] = high
        right_lo[s] = (value - high.astype(jnp.float32)).astype(jnp.bfloat16)

    def relay_slab(way):
        for n in range(per_way):
            slab_out(way * per_way + n).wait_recv()
            slab_on(way, n).start()

    def pass_slab(m):
        slab_direct(m).wait_recv()

        @pl.when(core == 0)
        def _():
            slab_pass(m, 2).start()

    half = rows_n // 4
    late = PASS_LATE

    def step(t, carried):
        for s in range(STEPS):
            for i in range(PARTS):
                steps = away[i, s]
                rising = steps <= reach[s]
                distance = jnp.where(rising, steps, rows_n - steps)
                j = t - jnp.where(
                    distance < half, distance * LAG, slots + (distance - half) * LAG
                )
                if i > 0:
                    j = j - LAGX

                @pl.when((j >= 0) & (j < chunks[i]))
                def _():
                    def arrived():
                        lift(i, s, j).wait_recv()

                    if i == 0:
                        pl.when(steps > 0)(arrived)
                    else:
                        arrived()

                    @pl.when(steps < reach[s])
                    def _():
                        lift(i, s, j).start()

                    @pl.when((steps == 0) | (steps > reach[s] + 1))
                    def _():
                        lower(i, s, j).start()

                    if i > 0:

                        @pl.when(steps > 0)
                        def _():
                            deliver(i, s, j).start()

        for m in range(FEEDS):

            @pl.when(t == m)
            def _():
                feed_slab(m)

            @pl.when(t == jnp.where(place == PARTS - 1, late + m, PASS_FROM + PASS_EVERY * m))
            def _():
                pass_slab(m)

        for way in range(PARTS - 1):

            @pl.when((t == RELAY_AT + RELAY_EVERY * way) & (place == way))
            def _():
                relay_slab(way)

        @pl.when(t == FEEDS)
        def _():
            split(0)

        return carried

    total_steps = max(
        2 * slots + LAG * (half + 1) + LAGX,
        PASS_FROM + PASS_EVERY * (FEEDS - 1) + 1,
        PASS_LATE + FEEDS,
        RELAY_AT + RELAY_EVERY * (PARTS - 2) + 1,
    )
    lax.fori_loop(0, total_steps, step, 0)

    for m in range(FEEDS):
        slab_pass(m, 0).wait_recv()
    split(1)
    split(2)

    for i in range(PARTS):
        for s in range(STEPS):
            if i > 0:

                @pl.when(away[0, s] > 0)
                def _():
                    deliver(i, s, 0, chunks[i]).wait_recv()

        at = pl.ds(begins[i], chunks[i] * ROWS)
        total = jnp.zeros((chunks[i] * ROWS, width), jnp.float32)
        for s in range(STEPS):
            value = left[s, at]
            high = value.astype(jnp.bfloat16)
            low = (value - high.astype(jnp.float32)).astype(jnp.bfloat16)
            for a, b in ((high, right_hi), (high, right_lo), (low, right_hi)):
                total = total + jnp.dot(a, b[s], preferred_element_type=jnp.float32)
        out_ref[at] = total

    for m in range(FEEDS):
        slab_direct(m).wait_send()
        slab_pass(m, 0).wait_send()
    for way in range(PARTS - 1):

        @pl.when(place == way)
        def _():
            for n in range(per_way):
                slab_on(way, n).wait_send()

    for s in range(STEPS):
        for i in range(PARTS):
            steps = away[i, s]

            @pl.when(steps < reach[s])
            def _():
                lift(i, s, 0, chunks[i]).wait_send()

            @pl.when((steps == 0) | (steps > reach[s] + 1))
            def _():
                lower(i, s, 0, chunks[i]).wait_send()

            if i > 0:

                @pl.when(steps > 0)
                def _():
                    deliver(i, s, 0, chunks[i]).wait_send()

                @pl.when(away[0, s] == 0)
                def _():
                    spread(i, s, 0, chunks[i]).wait_send()


def per_device(band, band_pattern, slab, slab_pattern):
    rows_n, cols_n = lax.axis_size("row"), lax.axis_size("col")
    height = band.shape[0]
    depth, width = slab.shape
    part = (height - OWN * ROWS) // (PARTS - 1)
    slots = max(OWN, part // ROWS)
    anywhere = pl.BlockSpec(memory_space=pl.ANY)
    dma = pltpu.SemaphoreType.DMA
    return pl.pallas_call(
        functools.partial(kernel, rows_n, cols_n),
        out_shape=jax.ShapeDtypeStruct((height, width), jnp.float32),
        in_specs=[anywhere] * 4,
        out_specs=pl.BlockSpec(memory_space=pltpu.VMEM),
        scratch_shapes=[
            pltpu.VMEM((STEPS, height, depth), jnp.float32),
            pltpu.VMEM((PARTS - 1, STEPS, part, depth), jnp.float32),
            pltpu.VMEM((STEPS, depth, width), jnp.float32),
            pltpu.VMEM((FEEDS // PARTS, depth // FEEDS, width), jnp.float32),
            pltpu.VMEM((STEPS, depth, width), jnp.bfloat16),
            pltpu.VMEM((STEPS, depth, width), jnp.bfloat16),
            pltpu.SMEM(band_pattern.shape, jnp.int32),
            pltpu.SMEM(slab_pattern.shape[::-1], jnp.int32),
            dma((STEPS + 3,)),
            dma((PARTS, STEPS, slots)),
            dma((PARTS, STEPS)),
            dma((PARTS, STEPS)),
            dma((PARTS - 1, STEPS)),
            dma((PARTS - 1, STEPS)),
            dma((PARTS - 1, STEPS)),
            dma((FEEDS,)),
            dma((FEEDS,)),
            dma((FEEDS // PARTS,)),
            dma((FEEDS // PARTS,)),
            dma((FEEDS,)),
            dma((FEEDS,)),
        ],
        compiler_params=pltpu.CompilerParams(
            collective_id=0, has_side_effects=True, vmem_limit_bytes=VMEM_MIB * 1024 * 1024
        ),
        cost_estimate=pl.CostEstimate(
            flops=2 * STEPS * height * depth * width,
            bytes_accessed=4 * (band.size + slab.size + height * width),
            transcendentals=0,
        ),
    )(band, band_pattern, slab, slab_pattern.T)


def solution(mesh):
    placed = (P("col", "row"), P("col", "row"), P("col", "row"), P("col", "row"))
    return jax.shard_map(
        per_device, mesh=mesh, in_specs=placed, out_specs=P("col", "row"), check_vma=False
    )
```

```python
import functools

import jax
import jax.numpy as jnp
from jax import lax
from jax.experimental import pallas as pl
from jax.experimental.pallas import tpu as pltpu
from jax.sharding import PartitionSpec as P

STEPS = 3
BLOCK = 128
PARTS = 4
ROWS = 8
CHUNKS = (18, 12, 6, 12)
LAG = 3
FAR = 12
LAGX = 1
LATE = (3,)
FEEDS = 8
RELAY_AT = (12, 14, 18)
FEED_AT = (0, 1, 2, 3, 4, 5, 12, 14)
PASS_FROM = 18
PASS_EVERY = 2
PASS_LATE = 37
VMEM_MIB = 53
MESH = pl.DeviceIdType.MESH


def kernel(
    rows_n,
    cols_n,
    band_ref,
    band_pattern_ref,
    slab_ref,
    slab_pattern_ref,
    out_ref,
    left,
    carry,
    right,
    through,
    right_hi,
    right_lo,
    band_keep,
    slab_keep,
    load_sem,
    stream_recv,
    up_send,
    down_send,
    side_send,
    spread_send,
    side_recv,
    slab_send,
    slab_recv,
    through_send,
    through_recv,
    pass_send,
    pass_recv,
):
    row = lax.axis_index("row")
    col = lax.axis_index("col")
    height, depth = left.shape[1], left.shape[2]
    width = right.shape[2]
    per_holder = band_ref.shape[1] // depth
    across = cols_n // PARTS
    chunks = CHUNKS
    begins = [sum(chunks[:i]) * ROWS for i in range(PARTS)]
    slots = max(chunks)
    core = lax.rem(col, 2)
    place = lax.rem(lax.div(col, 2), PARTS)
    sibling = col + 1 - 2 * core

    def column(offset):
        return lax.rem(col + (offset + cols_n), cols_n)

    up = lax.rem(row + 1, rows_n)
    down = lax.rem(row + rows_n - 1, rows_n)

    barrier = pltpu.get_barrier_semaphore()

    def greet(device):
        pl.semaphore_signal(barrier, inc=1, device_id=device, device_id_type=MESH)

    greet((up, col))
    greet((down, col))
    greet((row, sibling))
    greet((row, column(-2)))
    greet((row, column(2)))
    for k in range(1, PARTS):
        greet((row, column(across * k)))
    for where, offsets in ((0, (4, 6)), (1, (-4,)), (2, (-4, -6)), (3, (-6, 4, 6))):

        @pl.when(place == where)
        def _():
            for offset in offsets:
                greet((row, column(offset)))

    greetings = 8 + jnp.where(place == 3, 3, jnp.where(place == 1, 1, 2))

    inner, away = [], {}
    reach = [rows_n // 2, rows_n // 2 - 1 + core, rows_n // 2 - 1]
    for s in range(STEPS):
        for i in range(PARTS):
            group = lax.rem(column(-across * i) + s, cols_n)
            away[i, s] = lax.rem(row - lax.div(group, per_holder) + rows_n, rows_n)
            if i == 0:
                inner.append(lax.rem(group, per_holder))

    def piece_load(s):
        return pltpu.make_async_copy(
            band_ref.at[:, pl.ds(pl.multiple_of(inner[s] * depth, depth), depth)],
            left.at[s],
            load_sem.at[s],
        )

    def other_loads():
        return (
            pltpu.make_async_copy(slab_ref, right.at[0], load_sem.at[STEPS]),
            pltpu.make_async_copy(band_pattern_ref, band_keep, load_sem.at[STEPS + 1]),
            pltpu.make_async_copy(slab_pattern_ref, slab_keep, load_sem.at[STEPS + 2]),
        )

    for s in range(STEPS):

        @pl.when(away[0, s] == 0)
        def _():
            piece_load(s).start()

    for copy in other_loads():
        copy.start()
    for copy in other_loads()[1:]:
        copy.wait()

    pl.semaphore_wait(barrier, greetings)

    def held(i, s, j, count=1):
        if i == 0:
            return left.at[s, pl.ds(pl.multiple_of(j * ROWS, ROWS), count * ROWS)]
        return carry.at[
            i - 1, s, pl.ds(pl.multiple_of(j * ROWS, ROWS), count * ROWS)
        ]

    def settled(i, s, j, count=1):
        at = pl.ds(pl.multiple_of(begins[i] + j * ROWS, ROWS), count * ROWS)
        return left.at[s, at]

    def remote(source, target, send, recv, device):
        return pltpu.make_async_remote_copy(
            src_ref=source,
            dst_ref=target,
            send_sem=send,
            recv_sem=recv,
            device_id=device,
            device_id_type=MESH,
        )

    def lift(i, s, j, count=1):
        block = held(i, s, j, count)
        return remote(
            block, block, up_send.at[i, s], stream_recv.at[i, s, j], (up, col)
        )

    def lower(i, s, j, count=1):
        block = held(i, s, j, count)
        return remote(
            block, block, down_send.at[i, s], stream_recv.at[i, s, j], (down, col)
        )

    def deliver(i, s, j, count=1):
        return remote(
            held(i, s, j, count),
            settled(i, s, j, count),
            side_send.at[i - 1, s],
            side_recv.at[i - 1, s],
            (row, column(-across * i)),
        )

    def spread(i, s, j, count=1):
        return remote(
            settled(i, s, j, count),
            held(i, s, j, count),
            spread_send.at[i - 1, s],
            stream_recv.at[i, s, j],
            (row, column(across * i)),
        )

    def mask_band(i, s, j):
        rows = begins[i] + j * ROWS
        p = lax.div(rows, BLOCK)
        for q in range(depth // BLOCK):
            keep = band_keep[p, inner[s] * (depth // BLOCK) + q]
            at = (s, pl.ds(pl.multiple_of(rows, ROWS), ROWS), pl.ds(q * BLOCK, BLOCK))
            left[at] = left[at] * keep.astype(jnp.float32)

    feed = right.shape[1] // FEEDS
    per_way = FEEDS // PARTS

    def slab_rows(m):
        return pl.ds(m * feed, feed)

    def slab_direct(m):
        return remote(
            right.at[0, slab_rows(m)],
            right.at[2, slab_rows(m)],
            slab_send.at[m],
            slab_recv.at[m],
            (row, column(-2)),
        )

    def slab_out(m):
        way = m // per_way
        return remote(
            right.at[0, slab_rows(m)],
            through.at[m % per_way],
            slab_send.at[m],
            through_recv.at[m % per_way],
            (row, column(2 * way)),
        )

    def slab_on(way, n):
        m = way * per_way + n
        return remote(
            through.at[n],
            right.at[2, slab_rows(m)],
            through_send.at[n],
            slab_recv.at[m],
            (row, column(-2 * way - 2)),
        )

    def slab_pass(m, source):
        return remote(
            right.at[source, slab_rows(m)],
            right.at[1, slab_rows(m)],
            pass_send.at[m],
            pass_recv.at[m],
            (row, sibling),
        )

    other_loads()[0].wait()

    def feed_slab(m):
        for p in range(m * feed // BLOCK, -(-(m + 1) * feed // BLOCK)):
            first, last = max(m * feed, p * BLOCK), min((m + 1) * feed, (p + 1) * BLOCK)
            for n in range(width // BLOCK):
                keep = slab_keep[n, p]
                at = (0, pl.ds(first, last - first), pl.ds(n * BLOCK, BLOCK))
                right[at] = right[at] * keep.astype(jnp.float32)
        if m < per_way:
            slab_direct(m).start()
        else:

            @pl.when(place == 0)
            def _():
                slab_out(m).start()

            @pl.when(place > 0)
            def _():
                slab_direct(m).start()

        @pl.when(core == 1)
        def _():
            slab_pass(m, 0).start()

    def split(s):
        value = right[s]
        high = value.astype(jnp.bfloat16)
        right_hi[s] = high
        right_lo[s] = (value - high.astype(jnp.float32)).astype(jnp.bfloat16)

    def relay_slab(way):
        for n in range(per_way):
            slab_out(way * per_way + n).wait_recv()
            slab_on(way, n).start()

    def pass_slab(m):
        slab_direct(m).wait_recv()

        @pl.when(core == 0)
        def _():
            slab_pass(m, 2).start()

    half = rows_n // 4
    first = {}
    for i, s in away:
        steps = away[i, s]
        distance = jnp.where(steps <= reach[s], steps, rows_n - steps)
        first[i, s] = jnp.where(
            distance < half, distance * LAG, FAR + (distance - half) * LAG
        ) + (LAGX if i > 0 else 0)

    for s in range(STEPS):

        @pl.when(away[0, s] == 0)
        def _():
            piece_load(s).wait()

    late = PASS_LATE
    is_late = place == LATE[0]
    for other in LATE[1:]:
        is_late = is_late | (place == other)

    def step(t, carried):
        for s in range(STEPS):

            @pl.when((away[0, s] == 0) & (t < slots))
            def _():
                for i in range(PARTS):

                    @pl.when(t < chunks[i])
                    def _():
                        mask_band(i, s, t)
                        if i > 0:
                            spread(i, s, t).start()

        for s in range(STEPS):
            for i in range(PARTS):
                steps = away[i, s]
                j = t - first[i, s]

                @pl.when((j >= 0) & (j < chunks[i]))
                def _():
                    def arrived():
                        lift(i, s, j).wait_recv()

                    if i == 0:
                        pl.when(steps > 0)(arrived)
                    else:
                        arrived()

                    @pl.when(steps < reach[s])
                    def _():
                        lift(i, s, j).start()

                    @pl.when((steps == 0) | (steps > reach[s] + 1))
                    def _():
                        lower(i, s, j).start()

                    if i > 0:

                        @pl.when(steps > 0)
                        def _():
                            deliver(i, s, j).start()

        for n in range(FEEDS):
            m = (n + per_way) % FEEDS

            @pl.when(t == FEED_AT[n])
            def _():
                feed_slab(m)

            @pl.when(t == jnp.where(is_late, late + n, PASS_FROM + PASS_EVERY * n))
            def _():
                pass_slab(m)

        for way in range(1, PARTS):

            @pl.when((t == RELAY_AT[way - 1]) & (place == way))
            def _():
                relay_slab(way)

        @pl.when(t == FEED_AT[-1] + 1)
        def _():
            split(0)

        return carried

    total_steps = max(
        FAR + slots + LAG * (half + 1) + LAGX,
        PASS_FROM + PASS_EVERY * (FEEDS - 1) + 1,
        PASS_LATE + FEEDS,
        max(RELAY_AT) + 1,
    )
    lax.fori_loop(0, total_steps, step, 0)

    for m in range(FEEDS):
        slab_pass(m, 0).wait_recv()
    split(1)
    split(2)

    for i in range(PARTS):
        for s in range(STEPS):
            if i > 0:

                @pl.when(away[0, s] > 0)
                def _():
                    deliver(i, s, 0, chunks[i]).wait_recv()

        at = pl.ds(begins[i], chunks[i] * ROWS)
        total = jnp.zeros((chunks[i] * ROWS, width), jnp.float32)
        for s in range(STEPS):
            value = left[s, at]
            high = value.astype(jnp.bfloat16)
            low = (value - high.astype(jnp.float32)).astype(jnp.bfloat16)
            for a, b in ((high, right_hi), (high, right_lo), (low, right_hi)):
                total = total + jnp.dot(a, b[s], preferred_element_type=jnp.float32)
        out_ref[at] = total

    for m in range(FEEDS):
        slab_direct(m).wait_send()
        slab_pass(m, 0).wait_send()
    for way in range(1, PARTS):

        @pl.when(place == way)
        def _():
            for n in range(per_way):
                slab_on(way, n).wait_send()

    for s in range(STEPS):
        for i in range(PARTS):
            steps = away[i, s]

            @pl.when(steps < reach[s])
            def _():
                lift(i, s, 0, chunks[i]).wait_send()

            @pl.when((steps == 0) | (steps > reach[s] + 1))
            def _():
                lower(i, s, 0, chunks[i]).wait_send()

            if i > 0:

                @pl.when(steps > 0)
                def _():
                    deliver(i, s, 0, chunks[i]).wait_send()

                @pl.when(away[0, s] == 0)
                def _():
                    spread(i, s, 0, chunks[i]).wait_send()


def per_device(band, band_pattern, slab, slab_pattern):
    rows_n, cols_n = lax.axis_size("row"), lax.axis_size("col")
    height = band.shape[0]
    depth, width = slab.shape
    part = max(CHUNKS[1:]) * ROWS
    slots = max(CHUNKS)
    anywhere = pl.BlockSpec(memory_space=pl.ANY)
    dma = pltpu.SemaphoreType.DMA
    return pl.pallas_call(
        functools.partial(kernel, rows_n, cols_n),
        out_shape=jax.ShapeDtypeStruct((height, width), jnp.float32),
        in_specs=[anywhere] * 4,
        out_specs=pl.BlockSpec(memory_space=pltpu.VMEM),
        scratch_shapes=[
            pltpu.VMEM((STEPS, height, depth), jnp.float32),
            pltpu.VMEM((PARTS - 1, STEPS, part, depth), jnp.float32),
            pltpu.VMEM((STEPS, depth, width), jnp.float32),
            pltpu.VMEM((FEEDS // PARTS, depth // FEEDS, width), jnp.float32),
            pltpu.VMEM((STEPS, depth, width), jnp.bfloat16),
            pltpu.VMEM((STEPS, depth, width), jnp.bfloat16),
            pltpu.SMEM(band_pattern.shape, jnp.int32),
            pltpu.SMEM(slab_pattern.shape[::-1], jnp.int32),
            dma((STEPS + 3,)),
            dma((PARTS, STEPS, slots)),
            dma((PARTS, STEPS)),
            dma((PARTS, STEPS)),
            dma((PARTS - 1, STEPS)),
            dma((PARTS - 1, STEPS)),
            dma((PARTS - 1, STEPS)),
            dma((FEEDS,)),
            dma((FEEDS,)),
            dma((FEEDS // PARTS,)),
            dma((FEEDS // PARTS,)),
            dma((FEEDS,)),
            dma((FEEDS,)),
        ],
        compiler_params=pltpu.CompilerParams(
            collective_id=0, has_side_effects=True, vmem_limit_bytes=VMEM_MIB * 1024 * 1024
        ),
        cost_estimate=pl.CostEstimate(
            flops=2 * STEPS * height * depth * width,
            bytes_accessed=4 * (band.size + slab.size + height * width),
            transcendentals=0,
        ),
    )(band, band_pattern, slab, slab_pattern.T)


def solution(mesh):
    placed = (P("col", "row"), P("col", "row"), P("col", "row"), P("col", "row"))
    return jax.shard_map(
        per_device, mesh=mesh, in_specs=placed, out_specs=P("col", "row"), check_vma=False
    )
```

```python
import functools

import jax
import jax.numpy as jnp
from jax import lax
from jax.experimental import pallas as pl
from jax.experimental.pallas import tpu as pltpu
from jax.sharding import PartitionSpec as P

STEPS = 3
BLOCK = 128
PARTS = 4
ROWS = 8
CHUNKS = (18, 12, 6, 12)
SOON = (8, 6, 4, 6)
SOON_AT = 39
LAG = 3
FAR = 12
LAGX = 1
FEEDS = 8
RELAY_AT = (12, 14, 18)
FEED_AT = (0, 1, 2, 3, 4, 5, 16, 19)
PASS_FROM = 18
PASS_EVERY = 2
PASS_LATE = 31
VMEM_MIB = 53
MESH = pl.DeviceIdType.MESH


def kernel(
    rows_n,
    cols_n,
    band_ref,
    band_pattern_ref,
    slab_ref,
    slab_pattern_ref,
    out_ref,
    left,
    carry,
    right,
    through,
    right_hi,
    right_lo,
    band_keep,
    slab_keep,
    load_sem,
    stream_recv,
    up_send,
    down_send,
    side_send,
    spread_send,
    side_recv,
    slab_send,
    slab_recv,
    through_send,
    through_recv,
    pass_send,
    pass_recv,
):
    row = lax.axis_index("row")
    col = lax.axis_index("col")
    height, depth = left.shape[1], left.shape[2]
    width = right.shape[2]
    per_holder = band_ref.shape[1] // depth
    across = cols_n // PARTS
    chunks = CHUNKS
    begins = [sum(chunks[:i]) * ROWS for i in range(PARTS)]
    slots = max(chunks)
    core = lax.rem(col, 2)
    place = lax.rem(lax.div(col, 2), PARTS)
    sibling = col + 1 - 2 * core

    def column(offset):
        return lax.rem(col + (offset + cols_n), cols_n)

    up = lax.rem(row + 1, rows_n)
    down = lax.rem(row + rows_n - 1, rows_n)

    barrier = pltpu.get_barrier_semaphore()

    def greet(device):
        pl.semaphore_signal(barrier, inc=1, device_id=device, device_id_type=MESH)

    greet((up, col))
    greet((down, col))
    greet((row, sibling))
    greet((row, column(-2)))
    greet((row, column(2)))
    for k in range(1, PARTS):
        greet((row, column(across * k)))
    for where, offsets in ((0, (4, 6)), (1, (-4,)), (2, (-4, -6)), (3, (-6, 4, 6))):

        @pl.when(place == where)
        def _():
            for offset in offsets:
                greet((row, column(offset)))

    greetings = 8 + jnp.where(place == 3, 3, jnp.where(place == 1, 1, 2))

    inner, away = [], {}
    reach = [rows_n // 2, rows_n // 2 - 1 + core, rows_n // 2 - 1]
    for s in range(STEPS):
        for i in range(PARTS):
            group = lax.rem(column(-across * i) + s, cols_n)
            away[i, s] = lax.rem(row - lax.div(group, per_holder) + rows_n, rows_n)
            if i == 0:
                inner.append(lax.rem(group, per_holder))

    def piece_load(s):
        return pltpu.make_async_copy(
            band_ref.at[:, pl.ds(pl.multiple_of(inner[s] * depth, depth), depth)],
            left.at[s],
            load_sem.at[s],
        )

    def other_loads():
        return (
            pltpu.make_async_copy(slab_ref, right.at[0], load_sem.at[STEPS]),
            pltpu.make_async_copy(band_pattern_ref, band_keep, load_sem.at[STEPS + 1]),
            pltpu.make_async_copy(slab_pattern_ref, slab_keep, load_sem.at[STEPS + 2]),
        )

    for s in range(STEPS):

        @pl.when(away[0, s] == 0)
        def _():
            piece_load(s).start()

    for copy in other_loads():
        copy.start()
    for copy in other_loads()[1:]:
        copy.wait()

    pl.semaphore_wait(barrier, greetings)

    def held(i, s, j, count=1):
        if i == 0:
            return left.at[s, pl.ds(pl.multiple_of(j * ROWS, ROWS), count * ROWS)]
        return carry.at[
            i - 1, s, pl.ds(pl.multiple_of(j * ROWS, ROWS), count * ROWS)
        ]

    def settled(i, s, j, count=1):
        at = pl.ds(pl.multiple_of(begins[i] + j * ROWS, ROWS), count * ROWS)
        return left.at[s, at]

    def remote(source, target, send, recv, device):
        return pltpu.make_async_remote_copy(
            src_ref=source,
            dst_ref=target,
            send_sem=send,
            recv_sem=recv,
            device_id=device,
            device_id_type=MESH,
        )

    def lift(i, s, j, count=1):
        block = held(i, s, j, count)
        return remote(
            block, block, up_send.at[i, s], stream_recv.at[i, s, j], (up, col)
        )

    def lower(i, s, j, count=1):
        block = held(i, s, j, count)
        return remote(
            block, block, down_send.at[i, s], stream_recv.at[i, s, j], (down, col)
        )

    def deliver(i, s, j, count=1, tail=0):
        return remote(
            held(i, s, j, count),
            settled(i, s, j, count),
            side_send.at[i - 1, s],
            side_recv.at[i - 1, s, tail],
            (row, column(-across * i)),
        )

    def spread(i, s, j, count=1):
        return remote(
            settled(i, s, j, count),
            held(i, s, j, count),
            spread_send.at[i - 1, s],
            stream_recv.at[i, s, j],
            (row, column(across * i)),
        )

    def mask_band(i, s, j):
        rows = begins[i] + j * ROWS
        p = lax.div(rows, BLOCK)
        for q in range(depth // BLOCK):
            keep = band_keep[p, inner[s] * (depth // BLOCK) + q]
            at = (s, pl.ds(pl.multiple_of(rows, ROWS), ROWS), pl.ds(q * BLOCK, BLOCK))
            left[at] = left[at] * keep.astype(jnp.float32)

    feed = right.shape[1] // FEEDS
    per_way = FEEDS // PARTS

    def slab_rows(m):
        start = m * feed
        return pl.ds(start if isinstance(m, int) else pl.multiple_of(start, 8), feed)

    def slab_direct(m):
        return remote(
            right.at[0, slab_rows(m)],
            right.at[2, slab_rows(m)],
            slab_send.at[m],
            slab_recv.at[m],
            (row, column(-2)),
        )

    def slab_out(m):
        way = m // per_way
        return remote(
            right.at[0, slab_rows(m)],
            through.at[m % per_way],
            slab_send.at[m],
            through_recv.at[m % per_way],
            (row, column(2 * way)),
        )

    def slab_on(way, n):
        m = way * per_way + n
        return remote(
            through.at[n],
            right.at[2, slab_rows(m)],
            through_send.at[n],
            slab_recv.at[m],
            (row, column(-2 * way - 2)),
        )

    def slab_pass(m, source):
        return remote(
            right.at[source, slab_rows(m)],
            right.at[1, slab_rows(m)],
            pass_send.at[m],
            pass_recv.at[m],
            (row, sibling),
        )

    other_loads()[0].wait()

    def feed_slab(m):
        for p in range(m * feed // BLOCK, -(-(m + 1) * feed // BLOCK)):
            first, last = max(m * feed, p * BLOCK), min((m + 1) * feed, (p + 1) * BLOCK)
            for n in range(width // BLOCK):
                keep = slab_keep[n, p]
                at = (0, pl.ds(first, last - first), pl.ds(n * BLOCK, BLOCK))
                right[at] = right[at] * keep.astype(jnp.float32)
        if m < per_way:
            slab_direct(m).start()
        else:

            @pl.when(place == 0)
            def _():
                slab_out(m).start()

            @pl.when(place > 0)
            def _():
                slab_direct(m).start()

        @pl.when(core == 1)
        def _():
            slab_pass(m, 0).start()

    def split(s):
        value = right[s]
        high = value.astype(jnp.bfloat16)
        right_hi[s] = high
        right_lo[s] = (value - high.astype(jnp.float32)).astype(jnp.bfloat16)

    def multiply(s, tail):
        places = []
        for i in range(PARTS):
            j = SOON[i] if tail else 0
            count = chunks[i] - SOON[i] if tail else SOON[i]
            places.append(pl.ds(begins[i] + j * ROWS, count * ROWS))
            if i > 0:

                @pl.when(away[0, s] > 0)
                def _():
                    deliver(i, s, j, count, tail).wait_recv()

        value = jnp.concatenate([left[s, at] for at in places], axis=0)
        high = value.astype(jnp.bfloat16)
        low = (value - high.astype(jnp.float32)).astype(jnp.bfloat16)
        if s == 0:
            total = jnp.zeros((value.shape[0], width), jnp.float32)
        else:
            total = jnp.concatenate([out_ref[at] for at in places], axis=0)
        for a, b in ((high, right_hi), (high, right_lo), (low, right_hi)):
            total = total + jnp.dot(a, b[s], preferred_element_type=jnp.float32)
        begin = 0
        for at in places:
            out_ref[at] = total[begin : begin + at.size]
            begin += at.size

    def relay_slab(way):
        for n in range(per_way):
            slab_out(way * per_way + n).wait_recv()
            slab_on(way, n).start()

    def pass_slab(m):
        slab_direct(m).wait_recv()

        @pl.when(core == 0)
        def _():
            slab_pass(m, 2).start()

    half = rows_n // 4
    first = {}
    for i, s in away:
        steps = away[i, s]
        distance = jnp.where(steps <= reach[s], steps, rows_n - steps)
        first[i, s] = jnp.where(
            distance < half, distance * LAG, FAR + (distance - half) * LAG
        ) + (LAGX if i > 0 else 0)

    for s in range(STEPS):

        @pl.when(away[0, s] == 0)
        def _():
            piece_load(s).wait()

    pass_from = jnp.where(place == PARTS - 1, PASS_LATE, PASS_FROM)
    pass_every = jnp.where(place == PARTS - 1, 1, PASS_EVERY)
    relay_at = jnp.int32(-1)
    for way in range(1, PARTS):
        relay_at = jnp.where(place == way, RELAY_AT[way - 1], relay_at)
    is_holder = (away[0, 0] == 0) | (away[0, 1] == 0) | (away[0, 2] == 0)

    def step(t, carried):
        @pl.when(is_holder & (t < slots))
        def _():
            for s in range(STEPS):

                @pl.when(away[0, s] == 0)
                def _():
                    for i in range(PARTS):

                        @pl.when(t < chunks[i])
                        def _():
                            mask_band(i, s, t)
                            if i > 0:
                                spread(i, s, t).start()

        for s in range(STEPS):
            for i in range(PARTS):
                steps = away[i, s]
                j = t - first[i, s]

                @pl.when((j >= 0) & (j < chunks[i]))
                def _():
                    def arrived():
                        lift(i, s, j).wait_recv()

                    if i == 0:
                        pl.when(steps > 0)(arrived)
                    else:
                        arrived()

                    @pl.when(steps < reach[s])
                    def _():
                        lift(i, s, j).start()

                    @pl.when((steps == 0) | (steps > reach[s] + 1))
                    def _():
                        lower(i, s, j).start()

                    if i > 0:

                        @pl.when(steps > 0)
                        def _():
                            deliver(i, s, j, 1, jnp.where(j < SOON[i], 0, 1)).start()

        @pl.when(t <= FEED_AT[-1] + 1)
        def _():
            for n in range(FEEDS):

                @pl.when(t == FEED_AT[n])
                def _():
                    feed_slab((n + per_way) % FEEDS)

            @pl.when(t == FEED_AT[-1] + 1)
            def _():
                split(0)

        n = lax.div(t - pass_from, pass_every)

        @pl.when((t >= pass_from) & (n < FEEDS) & (n * pass_every == t - pass_from))
        def _():
            pass_slab(lax.rem(n + per_way, FEEDS))

        @pl.when((t >= min(RELAY_AT)) & (t == relay_at))
        def _():
            for way in range(1, PARTS):

                @pl.when(place == way)
                def _():
                    relay_slab(way)

        @pl.when(t >= SOON_AT)
        def _():
            for s in range(STEPS):

                @pl.when(t == SOON_AT + s)
                def _():
                    if s == 1:
                        for m in range(FEEDS):
                            slab_pass(m, 0).wait_recv()
                    if s > 0:
                        split(s)
                    multiply(s, 0)

        return carried

    total_steps = max(
        FAR + slots + LAG * (half + 1) + LAGX,
        PASS_FROM + PASS_EVERY * (FEEDS - 1) + 1,
        PASS_LATE + FEEDS,
        SOON_AT + STEPS,
        max(RELAY_AT) + 1,
    )
    lax.fori_loop(0, total_steps, step, 0)

    for s in range(STEPS):
        multiply(s, 1)

    for m in range(FEEDS):
        slab_direct(m).wait_send()
        slab_pass(m, 0).wait_send()
    for way in range(1, PARTS):

        @pl.when(place == way)
        def _():
            for n in range(per_way):
                slab_on(way, n).wait_send()

    for s in range(STEPS):
        for i in range(PARTS):
            steps = away[i, s]

            @pl.when(steps < reach[s])
            def _():
                lift(i, s, 0, chunks[i]).wait_send()

            @pl.when((steps == 0) | (steps > reach[s] + 1))
            def _():
                lower(i, s, 0, chunks[i]).wait_send()

            if i > 0:

                @pl.when(steps > 0)
                def _():
                    deliver(i, s, 0, chunks[i]).wait_send()

                @pl.when(away[0, s] == 0)
                def _():
                    spread(i, s, 0, chunks[i]).wait_send()


def per_device(band, band_pattern, slab, slab_pattern):
    rows_n, cols_n = lax.axis_size("row"), lax.axis_size("col")
    height = band.shape[0]
    depth, width = slab.shape
    part = max(CHUNKS[1:]) * ROWS
    slots = max(CHUNKS)
    anywhere = pl.BlockSpec(memory_space=pl.ANY)
    dma = pltpu.SemaphoreType.DMA
    return pl.pallas_call(
        functools.partial(kernel, rows_n, cols_n),
        out_shape=jax.ShapeDtypeStruct((height, width), jnp.float32),
        in_specs=[anywhere] * 4,
        out_specs=pl.BlockSpec(memory_space=pltpu.VMEM),
        scratch_shapes=[
            pltpu.VMEM((STEPS, height, depth), jnp.float32),
            pltpu.VMEM((PARTS - 1, STEPS, part, depth), jnp.float32),
            pltpu.VMEM((STEPS, depth, width), jnp.float32),
            pltpu.VMEM((FEEDS // PARTS, depth // FEEDS, width), jnp.float32),
            pltpu.VMEM((STEPS, depth, width), jnp.bfloat16),
            pltpu.VMEM((STEPS, depth, width), jnp.bfloat16),
            pltpu.SMEM(band_pattern.shape, jnp.int32),
            pltpu.SMEM(slab_pattern.shape[::-1], jnp.int32),
            dma((STEPS + 3,)),
            dma((PARTS, STEPS, slots)),
            dma((PARTS, STEPS)),
            dma((PARTS, STEPS)),
            dma((PARTS - 1, STEPS)),
            dma((PARTS - 1, STEPS)),
            dma((PARTS - 1, STEPS, 2)),
            dma((FEEDS,)),
            dma((FEEDS,)),
            dma((FEEDS // PARTS,)),
            dma((FEEDS // PARTS,)),
            dma((FEEDS,)),
            dma((FEEDS,)),
        ],
        compiler_params=pltpu.CompilerParams(
            collective_id=0, has_side_effects=True, vmem_limit_bytes=VMEM_MIB * 1024 * 1024
        ),
        cost_estimate=pl.CostEstimate(
            flops=2 * STEPS * height * depth * width,
            bytes_accessed=4 * (band.size + slab.size + height * width),
            transcendentals=0,
        ),
    )(band, band_pattern, slab, slab_pattern.T)


def solution(mesh):
    placed = (P("col", "row"), P("col", "row"), P("col", "row"), P("col", "row"))
    return jax.shard_map(
        per_device, mesh=mesh, in_specs=placed, out_specs=P("col", "row"), check_vma=False
    )
```

```python
import functools

import jax
import jax.numpy as jnp
from jax import lax
from jax.experimental import pallas as pl
from jax.experimental.pallas import tpu as pltpu
from jax.sharding import PartitionSpec as P

STEPS = 3
BLOCK = 128
PARTS = 4
ROWS = 8
CHUNKS = (18, 12, 6, 12)
SOON = (8, 6, 4, 6)
SOON_AT = 39
LAG = 3
FAR = 12
LAGX = 1
FEEDS = 8
RELAY_AT = (12, 14, 18)
FEED_AT = (0, 1, 2, 3, 4, 5, 16, 19)
PASS_FROM = 18
PASS_EVERY = 2
PASS_LATE = 31
VMEM_MIB = 53
MESH = pl.DeviceIdType.MESH


def kernel(
    rows_n,
    cols_n,
    band_ref,
    band_pattern_ref,
    slab_ref,
    slab_pattern_ref,
    out_ref,
    left,
    carry,
    right,
    through,
    right_hi,
    right_lo,
    band_keep,
    slab_keep,
    load_sem,
    stream_recv,
    up_send,
    down_send,
    side_send,
    spread_send,
    side_recv,
    slab_send,
    slab_recv,
    through_send,
    through_recv,
    pass_send,
    pass_recv,
):
    row = lax.axis_index("row")
    col = lax.axis_index("col")
    height, depth = left.shape[1], left.shape[2]
    width = right.shape[2]
    per_holder = band_ref.shape[1] // depth
    across = cols_n // PARTS
    chunks = CHUNKS
    begins = [sum(chunks[:i]) * ROWS for i in range(PARTS)]
    slots = max(chunks)
    core = lax.rem(col, 2)
    place = lax.rem(lax.div(col, 2), PARTS)
    sibling = col + 1 - 2 * core

    def column(offset):
        return lax.rem(col + (offset + cols_n), cols_n)

    up = lax.rem(row + 1, rows_n)
    down = lax.rem(row + rows_n - 1, rows_n)

    barrier = pltpu.get_barrier_semaphore()

    def greet(device):
        pl.semaphore_signal(barrier, inc=1, device_id=device, device_id_type=MESH)

    greet((up, col))
    greet((down, col))
    greet((row, sibling))
    greet((row, column(-2)))
    greet((row, column(2)))
    for k in range(1, PARTS):
        greet((row, column(across * k)))
    for where, offsets in ((0, (4, 6)), (1, (-4,)), (2, (-4, -6)), (3, (-6, 4, 6))):

        @pl.when(place == where)
        def _():
            for offset in offsets:
                greet((row, column(offset)))

    greetings = 8 + jnp.where(place == 3, 3, jnp.where(place == 1, 1, 2))

    inner, away = [], {}
    reach = [rows_n // 2, rows_n // 2 - 1 + core, rows_n // 2 - 1]
    for s in range(STEPS):
        for i in range(PARTS):
            group = lax.rem(column(-across * i) + s, cols_n)
            away[i, s] = lax.rem(row - lax.div(group, per_holder) + rows_n, rows_n)
            if i == 0:
                inner.append(lax.rem(group, per_holder))

    def piece_load(s):
        return pltpu.make_async_copy(
            band_ref.at[:, pl.ds(pl.multiple_of(inner[s] * depth, depth), depth)],
            left.at[s],
            load_sem.at[s],
        )

    def other_loads():
        return (
            pltpu.make_async_copy(slab_ref, right.at[0], load_sem.at[STEPS]),
            pltpu.make_async_copy(band_pattern_ref, band_keep, load_sem.at[STEPS + 1]),
            pltpu.make_async_copy(slab_pattern_ref, slab_keep, load_sem.at[STEPS + 2]),
        )

    for s in range(STEPS):

        @pl.when(away[0, s] == 0)
        def _():
            piece_load(s).start()

    for copy in other_loads():
        copy.start()
    for copy in other_loads()[1:]:
        copy.wait()

    pl.semaphore_wait(barrier, greetings)

    def held(i, s, j, count=1):
        if i == 0:
            return left.at[s, pl.ds(pl.multiple_of(j * ROWS, ROWS), count * ROWS)]
        return carry.at[
            i - 1, s, pl.ds(pl.multiple_of(j * ROWS, ROWS), count * ROWS)
        ]

    def settled(i, s, j, count=1):
        at = pl.ds(pl.multiple_of(begins[i] + j * ROWS, ROWS), count * ROWS)
        return left.at[s, at]

    def remote(source, target, send, recv, device):
        return pltpu.make_async_remote_copy(
            src_ref=source,
            dst_ref=target,
            send_sem=send,
            recv_sem=recv,
            device_id=device,
            device_id_type=MESH,
        )

    def lift(i, s, j, count=1):
        block = held(i, s, j, count)
        return remote(
            block, block, up_send.at[i, s], stream_recv.at[i, s, j], (up, col)
        )

    def lower(i, s, j, count=1):
        block = held(i, s, j, count)
        return remote(
            block, block, down_send.at[i, s], stream_recv.at[i, s, j], (down, col)
        )

    def deliver(i, s, j, count=1, tail=0):
        return remote(
            held(i, s, j, count),
            settled(i, s, j, count),
            side_send.at[i - 1, s],
            side_recv.at[i - 1, s, tail],
            (row, column(-across * i)),
        )

    def spread(i, s, j, count=1):
        return remote(
            settled(i, s, j, count),
            held(i, s, j, count),
            spread_send.at[i - 1, s],
            stream_recv.at[i, s, j],
            (row, column(across * i)),
        )

    def mask_band(i, s, j):
        rows = begins[i] + j * ROWS
        p = lax.div(rows, BLOCK)
        for q in range(depth // BLOCK):
            keep = band_keep[p, inner[s] * (depth // BLOCK) + q]
            at = (s, pl.ds(pl.multiple_of(rows, ROWS), ROWS), pl.ds(q * BLOCK, BLOCK))
            left[at] = left[at] * keep.astype(jnp.float32)

    feed = right.shape[1] // FEEDS
    per_way = FEEDS // PARTS

    def slab_rows(m):
        start = m * feed
        return pl.ds(start if isinstance(m, int) else pl.multiple_of(start, 8), feed)

    def slab_direct(m):
        return remote(
            right.at[0, slab_rows(m)],
            right.at[2, slab_rows(m)],
            slab_send.at[m],
            slab_recv.at[m],
            (row, column(-2)),
        )

    def slab_out(m):
        way = m // per_way
        return remote(
            right.at[0, slab_rows(m)],
            through.at[m % per_way],
            slab_send.at[m],
            through_recv.at[m % per_way],
            (row, column(2 * way)),
        )

    def slab_on(way, n):
        m = way * per_way + n
        return remote(
            through.at[n],
            right.at[2, slab_rows(m)],
            through_send.at[n],
            slab_recv.at[m],
            (row, column(-2 * way - 2)),
        )

    def slab_pass(m, source):
        return remote(
            right.at[source, slab_rows(m)],
            right.at[1, slab_rows(m)],
            pass_send.at[m],
            pass_recv.at[m],
            (row, sibling),
        )

    other_loads()[0].wait()

    def feed_slab(m):
        for p in range(m * feed // BLOCK, -(-(m + 1) * feed // BLOCK)):
            first, last = max(m * feed, p * BLOCK), min((m + 1) * feed, (p + 1) * BLOCK)
            for n in range(width // BLOCK):
                keep = slab_keep[n, p]
                at = (0, pl.ds(first, last - first), pl.ds(n * BLOCK, BLOCK))
                right[at] = right[at] * keep.astype(jnp.float32)
        if m < per_way:
            slab_direct(m).start()
        else:

            @pl.when(place == 0)
            def _():
                slab_out(m).start()

            @pl.when(place > 0)
            def _():
                slab_direct(m).start()

        @pl.when(core == 1)
        def _():
            slab_pass(m, 0).start()

    def split(s):
        value = right[s]
        high = value.astype(jnp.bfloat16)
        right_hi[s] = high
        right_lo[s] = (value - high.astype(jnp.float32)).astype(jnp.bfloat16)

    def multiply(s, tail):
        places = []
        for i in range(PARTS):
            j = SOON[i] if tail else 0
            count = chunks[i] - SOON[i] if tail else SOON[i]
            places.append(pl.ds(begins[i] + j * ROWS, count * ROWS))
            if i > 0:

                @pl.when(away[0, s] > 0)
                def _():
                    deliver(i, s, j, count, tail).wait_recv()

        value = jnp.concatenate([left[s, at] for at in places], axis=0)
        high = value.astype(jnp.bfloat16)
        low = (value - high.astype(jnp.float32)).astype(jnp.bfloat16)
        if s == 0:
            total = jnp.zeros((value.shape[0], width), jnp.float32)
        else:
            total = jnp.concatenate([out_ref[at] for at in places], axis=0)
        for a, b in ((high, right_hi), (high, right_lo), (low, right_hi)):
            total = total + jnp.dot(a, b[s], preferred_element_type=jnp.float32)
        begin = 0
        for at in places:
            out_ref[at] = total[begin : begin + at.size]
            begin += at.size

    def relay_slab(way):
        for n in range(per_way):
            slab_out(way * per_way + n).wait_recv()
            slab_on(way, n).start()

    def pass_slab(m):
        slab_direct(m).wait_recv()

        @pl.when(core == 0)
        def _():
            slab_pass(m, 2).start()

    half = rows_n // 4
    first, rises, falls, foreign = {}, {}, {}, {}
    for i, s in away:
        steps = away[i, s]
        distance = jnp.where(steps <= reach[s], steps, rows_n - steps)
        first[i, s] = jnp.where(
            distance < half, distance * LAG, FAR + (distance - half) * LAG
        ) + (LAGX if i > 0 else 0)
        rises[i, s] = steps < reach[s]
        falls[i, s] = (steps == 0) | (steps > reach[s] + 1)
        foreign[i, s] = steps > 0

    for s in range(STEPS):

        @pl.when(away[0, s] == 0)
        def _():
            piece_load(s).wait()

    pass_from = jnp.where(place == PARTS - 1, PASS_LATE, PASS_FROM)
    pass_every = jnp.where(place == PARTS - 1, 1, PASS_EVERY)
    relay_at = jnp.int32(-1)
    for way in range(1, PARTS):
        relay_at = jnp.where(place == way, RELAY_AT[way - 1], relay_at)
    is_holder = (away[0, 0] == 0) | (away[0, 1] == 0) | (away[0, 2] == 0)

    def step(t, carried):
        @pl.when(is_holder & (t < slots))
        def _():
            for s in range(STEPS):

                @pl.when(away[0, s] == 0)
                def _():
                    for i in range(PARTS):

                        @pl.when(t < chunks[i])
                        def _():
                            mask_band(i, s, t)
                            if i > 0:
                                spread(i, s, t).start()

        for s in range(STEPS):
            for i in range(PARTS):
                j = t - first[i, s]

                @pl.when((j >= 0) & (j < chunks[i]))
                def _():
                    def arrived():
                        lift(i, s, j).wait_recv()

                    if i == 0:
                        pl.when(foreign[i, s])(arrived)
                    else:
                        arrived()

                    @pl.when(rises[i, s])
                    def _():
                        lift(i, s, j).start()

                    @pl.when(falls[i, s])
                    def _():
                        lower(i, s, j).start()

                    if i > 0:

                        @pl.when(foreign[i, s])
                        def _():
                            deliver(i, s, j, 1, jnp.where(j < SOON[i], 0, 1)).start()

        @pl.when(t <= FEED_AT[-1] + 1)
        def _():
            for n in range(FEEDS):

                @pl.when(t == FEED_AT[n])
                def _():
                    feed_slab((n + per_way) % FEEDS)

            @pl.when(t == FEED_AT[-1] + 1)
            def _():
                split(0)

        n = lax.div(t - pass_from, pass_every)

        @pl.when((t >= pass_from) & (n < FEEDS) & (n * pass_every == t - pass_from))
        def _():
            pass_slab(lax.rem(n + per_way, FEEDS))

        @pl.when((t >= min(RELAY_AT)) & (t == relay_at))
        def _():
            for way in range(1, PARTS):

                @pl.when(place == way)
                def _():
                    relay_slab(way)

        @pl.when(t >= SOON_AT)
        def _():
            for s in range(STEPS):

                @pl.when(t == SOON_AT + s)
                def _():
                    if s == 1:
                        for m in range(FEEDS):
                            slab_pass(m, 0).wait_recv()
                    if s > 0:
                        split(s)
                    multiply(s, 0)

        return carried

    total_steps = max(
        FAR + LAG * half + max(chunks[0], max(chunks[1:]) + LAGX),
        PASS_FROM + PASS_EVERY * (FEEDS - 1) + 1,
        PASS_LATE + FEEDS,
        SOON_AT + STEPS,
        max(RELAY_AT) + 1,
    )
    lax.fori_loop(0, total_steps, step, 0)

    for s in range(STEPS):
        multiply(s, 1)

    for m in range(FEEDS):
        slab_direct(m).wait_send()
        slab_pass(m, 0).wait_send()
    for way in range(1, PARTS):

        @pl.when(place == way)
        def _():
            for n in range(per_way):
                slab_on(way, n).wait_send()

    for s in range(STEPS):
        for i in range(PARTS):
            steps = away[i, s]

            @pl.when(steps < reach[s])
            def _():
                lift(i, s, 0, chunks[i]).wait_send()

            @pl.when((steps == 0) | (steps > reach[s] + 1))
            def _():
                lower(i, s, 0, chunks[i]).wait_send()

            if i > 0:

                @pl.when(steps > 0)
                def _():
                    deliver(i, s, 0, chunks[i]).wait_send()

                @pl.when(away[0, s] == 0)
                def _():
                    spread(i, s, 0, chunks[i]).wait_send()


def per_device(band, band_pattern, slab, slab_pattern):
    rows_n, cols_n = lax.axis_size("row"), lax.axis_size("col")
    height = band.shape[0]
    depth, width = slab.shape
    part = max(CHUNKS[1:]) * ROWS
    slots = max(CHUNKS)
    anywhere = pl.BlockSpec(memory_space=pl.ANY)
    dma = pltpu.SemaphoreType.DMA
    return pl.pallas_call(
        functools.partial(kernel, rows_n, cols_n),
        out_shape=jax.ShapeDtypeStruct((height, width), jnp.float32),
        in_specs=[anywhere] * 4,
        out_specs=pl.BlockSpec(memory_space=pltpu.VMEM),
        scratch_shapes=[
            pltpu.VMEM((STEPS, height, depth), jnp.float32),
            pltpu.VMEM((PARTS - 1, STEPS, part, depth), jnp.float32),
            pltpu.VMEM((STEPS, depth, width), jnp.float32),
            pltpu.VMEM((FEEDS // PARTS, depth // FEEDS, width), jnp.float32),
            pltpu.VMEM((STEPS, depth, width), jnp.bfloat16),
            pltpu.VMEM((STEPS, depth, width), jnp.bfloat16),
            pltpu.SMEM(band_pattern.shape, jnp.int32),
            pltpu.SMEM(slab_pattern.shape[::-1], jnp.int32),
            dma((STEPS + 3,)),
            dma((PARTS, STEPS, slots)),
            dma((PARTS, STEPS)),
            dma((PARTS, STEPS)),
            dma((PARTS - 1, STEPS)),
            dma((PARTS - 1, STEPS)),
            dma((PARTS - 1, STEPS, 2)),
            dma((FEEDS,)),
            dma((FEEDS,)),
            dma((FEEDS // PARTS,)),
            dma((FEEDS // PARTS,)),
            dma((FEEDS,)),
            dma((FEEDS,)),
        ],
        compiler_params=pltpu.CompilerParams(
            collective_id=0, has_side_effects=True, vmem_limit_bytes=VMEM_MIB * 1024 * 1024
        ),
        cost_estimate=pl.CostEstimate(
            flops=2 * STEPS * height * depth * width,
            bytes_accessed=4 * (band.size + slab.size + height * width),
            transcendentals=0,
        ),
    )(band, band_pattern, slab, slab_pattern.T)


def solution(mesh):
    placed = (P("col", "row"), P("col", "row"), P("col", "row"), P("col", "row"))
    return jax.shard_map(
        per_device, mesh=mesh, in_specs=placed, out_specs=P("col", "row"), check_vma=False
    )
```
